32 devices in a mesh: groups: 2 (over x), dp: 8 (over z, y), tensor: 2 (over core).
Axes of the slice: x: 2, y: 2, z: 4, core: 2. Of those that a mesh axis runs over, the one named last changes fastest.
Arguments:
- inputs: bfloat16 [32, 128, 8192], P(('groups', 'dp'), None, 'tensor'), parts along dimension 0, may hold values from -6 to 6
- out_grads: bfloat16 [32, 128, 28672], P(('groups', 'dp'), None, 'tensor'), parts along dimension 0, may hold values from -6 to 6
- proj_in: bfloat16 [8192, 64], P('tensor'), may hold values from -0.0625 to 0.0625
- proj_out: bfloat16 [28672, 64], P('tensor'), may hold values from -0.03125 to 0.03125
- queries: bfloat16 [4096, 4096], P('tensor', 'dp'), may hold values from -1.1953125 to 1.1953125
Outputs:
- scores: float32 [32, 4096], P(('groups', 'dp'), 'tensor'), parts along dimension 0
The draws below stay inside these ranges and needn't reach their ends.
There are 2 independent parts, one for each index of `groups`. The reference program is written for one: setup_inputs(seed, part) draws one part's arguments, and reference() takes and returns one part's arrays. A program takes and returns all parts, laid end to end along the dimension named above; an argument that names none is the same for every part. Nothing has to cross between parts.
All inputs are finite; a program needn't handle non-finite values.
Results may differ from the reference program's by a relative error of at most 0.0029.
Values may be sent and summed in bfloat16 or wider, within the bound.
A program may use at most 64 MiB of HBM per device.

```python
import jax
import jax.numpy as jnp
from jax import lax

D_IN = 8192
D_OUT = 28672
RANK = 64
QUERIES = 4096
LEN = 128
EXAMPLES = 16


def shard_levels(rng, shape, pieces, low, largest):
    def one(axis_at, shards_of):
        heights = jax.random.uniform(jax.random.fold_in(jax.random.fold_in(rng, 6), axis_at), (shards_of,), jnp.float32, low / len(pieces), largest / len(pieces))
        return jnp.repeat(jnp.exp(heights), shape[axis_at] // shards_of).reshape((-1,) + (1,) * (len(shape) - axis_at - 1))

    level = one(*pieces[0])
    for cut in pieces[1:]:
        level = level * one(*cut)
    return level


def gaussian(own_key, shape, scale, bound, split=(), held_as=jnp.bfloat16):
    drawn = scale * jax.random.normal(own_key, shape, jnp.float32)
    if split:
        drawn = drawn * shard_levels(own_key, shape, split, -0.22, 0.18)
    return jnp.clip(drawn, -bound, bound).astype(held_as)


def setup_inputs(seed: int = 0, part: int = 0) -> dict:
    key_of = jax.random.split(jax.random.key(seed), 6)
    part_splits = jax.random.split(jax.random.fold_in(key_of[5], part), 6)
    return {
        "inputs": gaussian(part_splits[0], (EXAMPLES, LEN, D_IN), 1.0, 6.0, ((0, 8), (2, 2))),
        "out_grads": gaussian(part_splits[1], (EXAMPLES, LEN, D_OUT), 1.0, 6.0, ((0, 8), (2, 2))),
        "proj_in": gaussian(key_of[2], (D_IN, RANK), D_IN ** -0.5, 0.0625, ((0, 2),)),
        "proj_out": gaussian(key_of[3], (D_OUT, RANK), D_OUT ** -0.5, 0.03125, ((0, 2),)),
        "queries": gaussian(key_of[4], (QUERIES, RANK * RANK), 0.2, 1.1953125, ((0, 2), (1, 8))),
    }


def reference(inputs, out_grads, proj_in, proj_out, queries):
    a_in = jnp.dot(inputs.reshape(EXAMPLES * LEN, D_IN), proj_in, preferred_element_type=jnp.float32)
    a_out = jnp.dot(out_grads.reshape(EXAMPLES * LEN, D_OUT), proj_out, preferred_element_type=jnp.float32)
    a_in = a_in.reshape(EXAMPLES, LEN, RANK)
    a_out = a_out.reshape(EXAMPLES, LEN, RANK)
    sketch = jnp.einsum("elr,els->ers", a_out, a_in, precision=lax.Precision.HIGHEST) / LEN
    sketch_bf = sketch.reshape(EXAMPLES, RANK * RANK).astype(jnp.bfloat16)
    return jnp.dot(sketch_bf, queries.T, preferred_element_type=jnp.float32)
```

```python
import functools

import jax
import jax.numpy as jnp
from jax import lax
from jax.experimental import pallas as pl
from jax.experimental.pallas import tpu as pltpu
from jax.sharding import PartitionSpec as P

MESH = pl.DeviceIdType.MESH
LANES = 128
STRIPE = 2048
QUERY_CHUNKS = 2
NT = (((1,), (1,)), ((), ()))


def stripes(width):
    step = STRIPE if width % STRIPE == 0 else width
    return [(at, step) for at in range(0, width, step)]


def kernel(n, cores, examples, length, x_hbm, g_hbm, pi_hbm, po_hbm, q_hbm, out_ref,
           x, g, pi, po, q, in_mine, in_peer, outer, msg, got, entries, part, parts,
           load_sem, in_sem, msg_send, msg_recv, part_send, part_recv):
    me = lax.axis_index("dp")
    core = lax.axis_index("tensor")
    rank = pi.shape[0]
    tile = msg.shape[0] // n
    rows = rank // n
    pieces = rows * rank // LANES
    per_piece = LANES // rank

    def load(hbm, vmem, at, size, sem):
        return pltpu.make_async_copy(
            hbm.at[:, pl.ds(at, size)], vmem.at[:, pl.ds(at, size)], load_sem.at[sem])

    loads = []

    def start(hbm, vmem, at, size):
        copy = load(hbm, vmem, at, size, len(loads))
        copy.start()
        loads.append(copy)
        return copy

    in_loads = [(at, size, start(pi_hbm, pi, at, size), start(x_hbm, x, at, size))
                for at, size in stripes(x.shape[1])]
    out_loads = [(at, size, start(po_hbm, po, at, size), start(g_hbm, g, at, size))
                 for at, size in stripes(g.shape[1])]
    q_load = start(q_hbm, q, 0, q.shape[1])

    barrier = pltpu.get_barrier_semaphore()
    others = [(k, c) for k in range(n) for c in range(cores) if (k, c) != (0, 0)]

    def device(k, c):
        return {"dp": lax.rem(me + k, n), "tensor": lax.rem(core + c, cores)}

    for k, c in others:
        pl.semaphore_signal(barrier, inc=1, device_id=device(k, c), device_id_type=MESH)

    def project(proj, data, arrivals):
        total = None
        for at, size, first, second in arrivals:
            first.wait()
            second.wait()
            term = lax.dot_general(proj[:, pl.ds(at, size)], data[:, pl.ds(at, size)], NT,
                                   preferred_element_type=jnp.float32)
            total = term if total is None else total + term
        return total

    in_mine[...] = project(pi, x, in_loads)
    pl.semaphore_wait(barrier, len(others))
    swaps = []
    for c in range(1, cores):
        swap = pltpu.make_async_remote_copy(
            src_ref=in_mine, dst_ref=in_peer.at[c - 1], send_sem=in_sem.at[0, c - 1],
            recv_sem=in_sem.at[1, c - 1], device_id=device(0, c), device_id_type=MESH)
        swap.start()
        swaps.append(swap)
    out_side = project(po, g, out_loads)
    in_side = in_mine[...]
    for c, swap in enumerate(swaps):
        swap.wait()
        in_side = in_side + in_peer[c]

    for e in range(examples):
        tokens = slice(e * length, (e + 1) * length)
        outer[e] = lax.dot_general(out_side[:, tokens], in_side[:, tokens], NT,
                                   precision=lax.Precision.HIGHEST,
                                   preferred_element_type=jnp.float32)
    for e in range(examples):
        for j in range(pieces):
            joined = jnp.concatenate(
                [outer[e, pl.ds(per_piece * j + i, n, stride=rows), :] for i in range(per_piece)], 1)
            msg[pl.ds(e * pieces + j, n, stride=tile), :] = joined

    sends = []
    for k, c in others:
        to = pl.multiple_of(lax.rem(me + k, n) * tile, tile)
        copy = pltpu.make_async_remote_copy(
            src_ref=msg.at[pl.ds(to, tile)], dst_ref=got.at[c, pl.ds(k * tile, tile)],
            send_sem=msg_send.at[c, k], recv_sem=msg_recv.at[c, k],
            device_id=device(k, c), device_id_type=MESH)
        copy.start()
        sends.append(copy)
    got[0, pl.ds(0, tile)] = msg[pl.ds(pl.multiple_of(me * tile, tile), tile), :]
    q_load.wait()
    for copy in sends:
        copy.wait_recv()
    total = got[0]
    for c in range(1, cores):
        total = total + got[c]
    entries[...] = total * (1.0 / length)
    sketch = jnp.concatenate(
        [jnp.concatenate([entries[pl.ds(e * pieces + j, n, stride=tile), :] for e in range(examples)], 0)
         for j in range(pieces)], 1).astype(jnp.bfloat16)

    queries_here = q.shape[0]
    chunk = queries_here // QUERY_CHUNKS
    blocks = chunk // LANES
    height = blocks * examples
    final = []
    for h in range(QUERY_CHUNKS):
        scores = lax.dot_general(sketch, q[pl.ds(h * chunk, chunk), :], NT,
                                 preferred_element_type=jnp.float32)
        for b in range(blocks):
            for e in range(examples):
                part[pl.ds(h * n * height + b * examples + e, n, stride=height), :] = (
                    scores[e * n:(e + 1) * n, b * LANES:(b + 1) * LANES])
        for k in range(1, n):
            at = pl.ds((h * n + k) * height, height)
            copy = pltpu.make_async_remote_copy(
                src_ref=part.at[at], dst_ref=parts.at[at],
                send_sem=part_send.at[h, k], recv_sem=part_recv.at[h, k],
                device_id=device(n - k, 0), device_id_type=MESH)
            copy.start()
            final.append(copy)
    for h in range(QUERY_CHUNKS):
        total = part[pl.ds(h * n * height, height), :]
        for k in range(1, n):
            final[h * (n - 1) + k - 1].wait_recv()
            total = total + parts[pl.ds((h * n + k) * height, height), :]
        out_ref[pl.ds(h * height, height), :] = total
    for copy in sends + final:
        copy.wait_send()


def on_device(n, cores, inputs, out_grads, proj_in, proj_out, queries):
    examples, length, d_in = inputs.shape
    d_out = out_grads.shape[2]
    rank = proj_in.shape[1]
    queries_here, entries_here = queries.shape
    tokens = examples * length
    tile = max(8, examples * entries_here // LANES)
    out_rows = examples * queries_here // LANES
    f32, bf16 = jnp.float32, jnp.bfloat16
    n_loads = 2 * len(stripes(d_in)) + 2 * len(stripes(d_out)) + 1
    dma = pltpu.SemaphoreType.DMA
    flat = pl.pallas_call(
        functools.partial(kernel, n, cores, examples, length),
        out_shape=jax.ShapeDtypeStruct((out_rows, LANES), f32),
        in_specs=[pl.BlockSpec(memory_space=pl.ANY)] * 5,
        out_specs=pl.BlockSpec(memory_space=pltpu.VMEM),
        scratch_shapes=[
            pltpu.VMEM((tokens, d_in), bf16),
            pltpu.VMEM((tokens, d_out), bf16),
            pltpu.VMEM((rank, d_in), bf16),
            pltpu.VMEM((rank, d_out), bf16),
            pltpu.VMEM((queries_here, entries_here), bf16),
            pltpu.VMEM((rank, tokens), f32),
            pltpu.VMEM((cores - 1, rank, tokens), f32),
            pltpu.VMEM((examples, rank, rank), f32),
            pltpu.VMEM((n * tile, LANES), f32),
            pltpu.VMEM((cores, n * tile, LANES), f32),
            pltpu.VMEM((n * tile, LANES), f32),
            pltpu.VMEM((n * out_rows, LANES), f32),
            pltpu.VMEM((n * out_rows, LANES), f32),
            dma((n_loads,)),
            dma((2, cores - 1)),
            dma((cores, n)),
            dma((cores, n)),
            dma((QUERY_CHUNKS, n)),
            dma((QUERY_CHUNKS, n)),
        ],
        compiler_params=pltpu.CompilerParams(
            collective_id=0, has_side_effects=True, vmem_limit_bytes=40 * 2**20),
    )(inputs.reshape(tokens, d_in), out_grads.reshape(tokens, d_out), proj_in.T, proj_out.T, queries)
    return flat.reshape(queries_here // LANES, examples, LANES).transpose(1, 0, 2).reshape(
        examples, queries_here)


def solution(mesh):
    return jax.shard_map(
        functools.partial(on_device, mesh.shape["dp"], mesh.shape["tensor"]),
        mesh=mesh,
        in_specs=(
            P(("groups", "dp"), None, "tensor"),
            P(("groups", "dp"), None, "tensor"),
            P("tensor", None),
            P("tensor", None),
            P("tensor", "dp"),
        ),
        out_specs=P(("groups", "dp"), "tensor"),
        check_vma=False,
    )
```

```python
import functools

import jax
import jax.numpy as jnp
from jax import lax
from jax.experimental import pallas as pl
from jax.experimental.pallas import tpu as pltpu
from jax.sharding import PartitionSpec as P

MESH = pl.DeviceIdType.MESH
LANES = 128
STRIPE = 2048
QUERY_CHUNKS = 1
NT = (((1,), (1,)), ((), ()))


def stripes(width):
    step = STRIPE if width % STRIPE == 0 else width
    return [(at, step) for at in range(0, width, step)]


def kernel(n, cores, examples, length, x_hbm, g_hbm, pi_hbm, po_hbm, q_hbm, out_ref,
           x, g, pi, po, q, in_mine, in_peer, outer, msg, got, entries, wide, parts,
           load_sem, in_sem, msg_send, msg_recv, part_send, part_recv):
    me = lax.axis_index("dp")
    core = lax.axis_index("tensor")
    rank = pi.shape[0]
    tokens = x.shape[0]
    pieces = msg.shape[2]
    per_piece = LANES // rank

    loads = []

    def start(hbm, vmem, row, height, at, size):
        where = (pl.ds(row, height), pl.ds(at, size))
        copy = pltpu.make_async_copy(hbm.at[where], vmem.at[where], load_sem.at[len(loads)])
        copy.start()
        loads.append(copy)
        return copy

    in_loads = [(at, size, (start(pi_hbm, pi, 0, rank, at, size), start(x_hbm, x, 0, tokens, at, size)))
                for at, size in stripes(x.shape[1])]
    out_loads = []
    for e in range(examples):
        arrivals = []
        for at, size in stripes(g.shape[1]):
            copies = (start(po_hbm, po, 0, rank, at, size),) if e == 0 else ()
            arrivals.append((at, size, copies + (start(g_hbm, g, e * length, length, at, size),)))
        out_loads.append(arrivals)
    q_load = start(q_hbm, q, 0, q.shape[0], 0, q.shape[1])

    barrier = pltpu.get_barrier_semaphore()
    others = [(k, c) for k in range(n) for c in range(cores) if (k, c) != (0, 0)]

    def device(k, c):
        return {"dp": lax.rem(me + k, n), "tensor": lax.rem(core + c, cores)}

    for k, c in others:
        pl.semaphore_signal(barrier, inc=1, device_id=device(k, c), device_id_type=MESH)

    def project(proj, data, row, height, arrivals):
        total = None
        for at, size, copies in arrivals:
            for copy in copies:
                copy.wait()
            term = lax.dot_general(proj[:, pl.ds(at, size)], data[pl.ds(row, height), pl.ds(at, size)],
                                   NT, preferred_element_type=jnp.float32)
            total = term if total is None else total + term
        return total

    in_mine[...] = project(pi, x, 0, tokens, in_loads)
    pl.semaphore_wait(barrier, len(others))
    swaps = []
    for c in range(1, cores):
        swap = pltpu.make_async_remote_copy(
            src_ref=in_mine, dst_ref=in_peer.at[c - 1], send_sem=in_sem.at[0, c - 1],
            recv_sem=in_sem.at[1, c - 1], device_id=device(0, c), device_id_type=MESH)
        swap.start()
        swaps.append(swap)

    sends = []
    in_side = None
    for e in range(examples):
        out_side = project(po, g, e * length, length, out_loads[e])
        if in_side is None:
            in_side = in_mine[...]
            for c, swap in enumerate(swaps):
                swap.wait()
                in_side = in_side + in_peer[c]
        outer[e] = lax.dot_general(out_side, in_side[:, e * length:(e + 1) * length], NT,
                                   precision=lax.Precision.HIGHEST,
                                   preferred_element_type=jnp.float32)
        joined = jnp.concatenate(
            [outer[e, pl.ds(i, rank // per_piece, stride=per_piece), :] for i in range(per_piece)], 1)
        for d in range(n):
            msg[e, d] = joined[d * pieces:(d + 1) * pieces]
        copies = []
        for k, c in others:
            copy = pltpu.make_async_remote_copy(
                src_ref=msg.at[e, lax.rem(me + k, n)], dst_ref=got.at[e, c, k],
                send_sem=msg_send.at[e, c, k], recv_sem=msg_recv.at[e, c, k],
                device_id=device(k, c), device_id_type=MESH)
            copy.start()
            copies.append(copy)
        sends.append(copies)

    q_load.wait()
    queries_here = q.shape[0]
    chunk = queries_here // QUERY_CHUNKS
    blocks = chunk // LANES
    final = {}
    for e in range(examples):
        got[e, 0, 0] = msg[e, me]
        for copy in sends[e]:
            copy.wait_recv()
        for k in range(n):
            total = got[e, 0, k]
            for c in range(1, cores):
                total = total + got[e, c, k]
            entries[e, pl.ds(k * pieces, pieces), :] = total * (1.0 / length)
        sketch = jnp.concatenate(
            [entries[e, pl.ds(j, n, stride=pieces), :] for j in range(pieces)], 1).astype(jnp.bfloat16)
        for h in range(QUERY_CHUNKS):
            scores = lax.dot_general(sketch, q[pl.ds(h * chunk, chunk), :], NT,
                                     preferred_element_type=jnp.float32)
            for b in range(blocks):
                wide[e, h, pl.ds(b, n, stride=blocks), :] = scores[:, b * LANES:(b + 1) * LANES]
            for k in range(1, n):
                copy = pltpu.make_async_remote_copy(
                    src_ref=wide.at[e, h, pl.ds(k * blocks, blocks)], dst_ref=parts.at[e, h, k],
                    send_sem=part_send.at[e, h, k], recv_sem=part_recv.at[e, h, k],
                    device_id=device(n - k, 0), device_id_type=MESH)
                copy.start()
                final[e, h, k] = copy
    for e in range(examples):
        for h in range(QUERY_CHUNKS):
            total = wide[e, h, pl.ds(0, blocks), :]
            for k in range(1, n):
                final[e, h, k].wait_recv()
                total = total + parts[e, h, k].astype(jnp.float32)
            out_ref[pl.ds(h * blocks * examples + e, blocks, stride=examples), :] = total
    for copies in sends:
        for copy in copies:
            copy.wait_send()
    for copy in final.values():
        copy.wait_send()


def on_device(n, cores, inputs, out_grads, proj_in, proj_out, queries):
    examples, length, d_in = inputs.shape
    d_out = out_grads.shape[2]
    rank = proj_in.shape[1]
    queries_here, entries_here = queries.shape
    tokens = examples * length
    pieces = entries_here // LANES
    out_rows = examples * queries_here // LANES
    blocks = queries_here // QUERY_CHUNKS // LANES
    f32, bf16 = jnp.float32, jnp.bfloat16
    n_loads = 2 * len(stripes(d_in)) + (1 + examples) * len(stripes(d_out)) + 1
    dma = pltpu.SemaphoreType.DMA
    flat = pl.pallas_call(
        functools.partial(kernel, n, cores, examples, length),
        out_shape=jax.ShapeDtypeStruct((out_rows, LANES), f32),
        in_specs=[pl.BlockSpec(memory_space=pl.ANY)] * 5,
        out_specs=pl.BlockSpec(memory_space=pltpu.VMEM),
        scratch_shapes=[
            pltpu.VMEM((tokens, d_in), bf16),
            pltpu.VMEM((tokens, d_out), bf16),
            pltpu.VMEM((rank, d_in), bf16),
            pltpu.VMEM((rank, d_out), bf16),
            pltpu.VMEM((queries_here, entries_here), bf16),
            pltpu.VMEM((rank, tokens), f32),
            pltpu.VMEM((cores - 1, rank, tokens), f32),
            pltpu.VMEM((examples, rank, rank), f32),
            pltpu.VMEM((examples, n, pieces, LANES), f32),
            pltpu.VMEM((examples, cores, n, pieces, LANES), f32),
            pltpu.VMEM((examples, n * pieces, LANES), f32),
            pltpu.VMEM((examples, QUERY_CHUNKS, n * blocks, LANES), f32),
            pltpu.VMEM((examples, QUERY_CHUNKS, n, blocks, LANES), f32),
            dma((n_loads,)),
            dma((2, cores - 1)),
            dma((examples, cores, n)),
            dma((examples, cores, n)),
            dma((examples, QUERY_CHUNKS, n)),
            dma((examples, QUERY_CHUNKS, n)),
        ],
        compiler_params=pltpu.CompilerParams(
            collective_id=0, has_side_effects=True, vmem_limit_bytes=60 * 2**20),
    )(inputs.reshape(tokens, d_in), out_grads.reshape(tokens, d_out), proj_in.T, proj_out.T, queries)
    return flat.reshape(queries_here // LANES, examples, LANES).transpose(1, 0, 2).reshape(
        examples, queries_here)


def solution(mesh):
    return jax.shard_map(
        functools.partial(on_device, mesh.shape["dp"], mesh.shape["tensor"]),
        mesh=mesh,
        in_specs=(
            P(("groups", "dp"), None, "tensor"),
            P(("groups", "dp"), None, "tensor"),
            P("tensor", None),
            P("tensor", None),
            P("tensor", "dp"),
        ),
        out_specs=P(("groups", "dp"), "tensor"),
        check_vma=False,
    )
```

```python
import functools

import jax
import jax.numpy as jnp
from jax import lax
from jax.experimental import pallas as pl
from jax.experimental.pallas import tpu as pltpu
from jax.sharding import PartitionSpec as P

MESH = pl.DeviceIdType.MESH
LANES = 128
STRIPE = 2048
IN_FLIGHT = 10
QUERY_CHUNKS = 2
NT = (((1,), (1,)), ((), ()))


def stripes(width):
    step = STRIPE if width % STRIPE == 0 else width
    return [(at, step) for at in range(0, width, step)]


def kernel(n, cores, examples, length, x_hbm, g_hbm, pi_hbm, po_hbm, q_hbm, out_ref,
           x, g, pi, po, q, in_mine, in_peer, outer, share, share_peer, msg, got, entries, wide, part, parts,
           load_sem, in_sem, share_sem, msg_send, msg_recv, part_send, part_recv):
    me = lax.axis_index("dp")
    core = lax.axis_index("tensor")
    rank = pi.shape[0]
    tokens = x.shape[0]
    tile = msg.shape[1]
    pieces = tile // examples
    per_piece = LANES // rank

    loads = []

    def plan(hbm, vmem, row, height, at, size):
        where = (pl.ds(row, height), pl.ds(at, size))
        copy = pltpu.make_async_copy(hbm.at[where], vmem.at[where], load_sem.at[len(loads)])
        loads.append(copy)
        return len(loads) - 1

    in_loads = [(at, size, (plan(pi_hbm, pi, 0, rank, at, size), plan(x_hbm, x, 0, tokens, at, size)))
                for at, size in stripes(x.shape[1])]
    out_loads = [(at, size, (plan(po_hbm, po, 0, rank, at, size), plan(g_hbm, g, 0, tokens, at, size)))
                 for at, size in stripes(g.shape[1])]
    q_load = plan(q_hbm, q, 0, q.shape[0], 0, q.shape[1])

    for copy in loads[:IN_FLIGHT]:
        copy.start()

    def arrive(at):
        loads[at].wait()
        if at + IN_FLIGHT < len(loads):
            loads[at + IN_FLIGHT].start()

    barrier = pltpu.get_barrier_semaphore()
    others = [(k, 0) for k in range(1, n)] + [(0, c) for c in range(1, cores)]

    def device(k, c):
        return {"dp": lax.rem(me + k, n), "tensor": lax.rem(core + c, cores)}

    for k, c in others:
        pl.semaphore_signal(barrier, inc=1, device_id=device(k, c), device_id_type=MESH)

    def by_token(proj, data):
        return lax.dot_general(data, proj, NT, preferred_element_type=jnp.float32)

    def halves(value):
        high = value.astype(jnp.bfloat16)
        return high, (value - high.astype(jnp.float32)).astype(jnp.bfloat16)

    def project(multiply, proj, data, row, height, arrivals):
        total = None
        for at, size, copies in arrivals:
            for copy in copies:
                arrive(copy)
            term = multiply(proj[:, pl.ds(at, size)], data[pl.ds(row, height), pl.ds(at, size)])
            total = term if total is None else total + term
        return total

    mine = project(by_token, pi, x, 0, tokens, in_loads)
    in_mine[...] = jnp.concatenate(
        [mine[e * length:(e + 1) * length] for e in range(examples)], 1)

    before = len(out_loads) // 2
    out_side = project(by_token, po, g, 0, tokens, out_loads[:before]) if before else 0.0
    pl.semaphore_wait(barrier, len(others))

    def swap(source, peers, sems):
        copies = [
            pltpu.make_async_remote_copy(
                src_ref=source, dst_ref=peers.at[c - 1], send_sem=sems.at[0, c - 1],
                recv_sem=sems.at[1, c - 1], device_id=device(0, c), device_id_type=MESH)
            for c in range(1, cores)]
        for copy in copies:
            copy.start()
        return copies

    in_swap = swap(in_mine, in_peer, in_sem)
    out_side = out_side + project(by_token, po, g, 0, tokens, out_loads[before:])
    out_high, out_low = halves(out_side.T)
    in_side = in_mine[...]
    for c, copy in enumerate(in_swap):
        copy.wait()
        in_side = in_side + in_peer[c]
    in_high, in_low = halves(in_side)

    half = rank // per_piece
    for e in range(examples):
        here, there = slice(e * length, (e + 1) * length), slice(e * rank, (e + 1) * rank)
        left_high, left_low = out_high[:, here], out_low[:, here]
        high, low = in_high[:, there], in_low[:, there]
        outer[e] = jnp.dot(jnp.concatenate([left_high, left_high, left_low, left_low], 1),
                           jnp.concatenate([high, low, high, low], 0),
                           preferred_element_type=jnp.float32)
        share[pl.ds(e * half, half), :] = jnp.concatenate(
            [outer[e, pl.ds(i, half, stride=per_piece), :] for i in range(per_piece)], 1)
    share_swap = swap(share, share_peer, share_sem)
    joined = share[...]
    for c, copy in enumerate(share_swap):
        copy.wait()
        joined = joined + share_peer[c]
    joined = joined * (1.0 / length)
    for d in range(n):
        for e in range(examples):
            msg[d, pl.ds(e * pieces, pieces), :] = joined[e * half + d * pieces:e * half + (d + 1) * pieces]
    sends = []
    for k in range(1, n):
        copy = pltpu.make_async_remote_copy(
            src_ref=msg.at[lax.rem(me + k, n)], dst_ref=got.at[k],
            send_sem=msg_send.at[k], recv_sem=msg_recv.at[k],
            device_id=device(k, 0), device_id_type=MESH)
        copy.start()
        sends.append(copy)
    arrive(q_load)
    entries[pl.ds(0, tile), :] = msg[me]
    for k in range(1, n):
        sends[k - 1].wait_recv()
        entries[pl.ds(k * tile, tile), :] = got[k]
    sketch = jnp.concatenate(
        [jnp.concatenate([entries[pl.ds(e * pieces + j, n, stride=tile), :] for e in range(examples)], 0)
         for j in range(pieces)], 1).astype(jnp.bfloat16)

    chunk = q.shape[0] // QUERY_CHUNKS
    blocks = chunk // LANES
    height = blocks * examples
    final = {}
    for h in range(QUERY_CHUNKS):
        scores = lax.dot_general(sketch, q[pl.ds(h * chunk, chunk), :], NT,
                                 preferred_element_type=jnp.float32)
        for b in range(blocks):
            for e in range(examples):
                wide[h, pl.ds(b * examples + e, n, stride=height), :] = (
                    scores[e * n:(e + 1) * n, b * LANES:(b + 1) * LANES])
        for k in range(1, n):
            part[h, k] = wide[h, pl.ds(k * height, height), :].astype(part.dtype)
            copy = pltpu.make_async_remote_copy(
                src_ref=part.at[h, k], dst_ref=parts.at[h, k],
                send_sem=part_send.at[h, k], recv_sem=part_recv.at[h, k],
                device_id=device(n - k, 0), device_id_type=MESH)
            copy.start()
            final[h, k] = copy
    for h in range(QUERY_CHUNKS):
        total = wide[h, pl.ds(0, height), :]
        for k in range(1, n):
            final[h, k].wait_recv()
            total = total + parts[h, k].astype(jnp.float32)
        out_ref[pl.ds(h * height, height), :] = total
    for copy in sends + list(final.values()):
        copy.wait_send()


def on_device(n, cores, inputs, out_grads, proj_in, proj_out, queries):
    examples, length, d_in = inputs.shape
    d_out = out_grads.shape[2]
    rank = proj_in.shape[1]
    queries_here, entries_here = queries.shape
    tokens = examples * length
    pieces = entries_here // LANES
    out_rows = examples * queries_here // LANES
    blocks = queries_here // QUERY_CHUNKS // LANES
    f32, bf16 = jnp.float32, jnp.bfloat16
    n_loads = 2 * len(stripes(d_in)) + 2 * len(stripes(d_out)) + 1
    dma = pltpu.SemaphoreType.DMA
    flat = pl.pallas_call(
        functools.partial(kernel, n, cores, examples, length),
        out_shape=jax.ShapeDtypeStruct((out_rows, LANES), f32),
        in_specs=[pl.BlockSpec(memory_space=pl.ANY)] * 5,
        out_specs=pl.BlockSpec(memory_space=pltpu.VMEM),
        scratch_shapes=[
            pltpu.VMEM((tokens, d_in), bf16),
            pltpu.VMEM((tokens, d_out), bf16),
            pltpu.VMEM((rank, d_in), bf16),
            pltpu.VMEM((rank, d_out), bf16),
            pltpu.VMEM((queries_here, entries_here), bf16),
            pltpu.VMEM((length, examples * rank), f32),
            pltpu.VMEM((cores - 1, length, examples * rank), f32),
            pltpu.VMEM((examples, rank, rank), f32),
            pltpu.VMEM((examples * pieces * n, LANES), f32),
            pltpu.VMEM((cores - 1, examples * pieces * n, LANES), f32),
            pltpu.VMEM((n, examples * pieces, LANES), f32),
            pltpu.VMEM((n, examples * pieces, LANES), f32),
            pltpu.VMEM((n * examples * pieces, LANES), f32),
            pltpu.VMEM((QUERY_CHUNKS, n * examples * blocks, LANES), f32),
            pltpu.VMEM((QUERY_CHUNKS, n, examples * blocks, LANES), bf16),
            pltpu.VMEM((QUERY_CHUNKS, n, examples * blocks, LANES), bf16),
            dma((n_loads,)),
            dma((2, cores - 1)),
            dma((2, cores - 1)),
            dma((n,)),
            dma((n,)),
            dma((QUERY_CHUNKS, n)),
            dma((QUERY_CHUNKS, n)),
        ],
        compiler_params=pltpu.CompilerParams(
            collective_id=0, has_side_effects=True, vmem_limit_bytes=60 * 2**20),
    )(inputs.reshape(tokens, d_in), out_grads.reshape(tokens, d_out), proj_in.T, proj_out.T, queries)
    return flat.reshape(queries_here // LANES, examples, LANES).transpose(1, 0, 2).reshape(
        examples, queries_here)


def solution(mesh):
    return jax.shard_map(
        functools.partial(on_device, mesh.shape["dp"], mesh.shape["tensor"]),
        mesh=mesh,
        in_specs=(
            P(("groups", "dp"), None, "tensor"),
            P(("groups", "dp"), None, "tensor"),
            P("tensor", None),
            P("tensor", None),
            P("tensor", "dp"),
        ),
        out_specs=P(("groups", "dp"), "tensor"),
        check_vma=False,
    )
```

```python
import functools

import jax
import jax.numpy as jnp
from jax import lax
from jax.experimental import pallas as pl
from jax.experimental.pallas import tpu as pltpu
from jax.sharding import PartitionSpec as P

MESH = pl.DeviceIdType.MESH
LANES = 128
STRIPE = 2048
IN_FLIGHT = 100
QUERY_CHUNKS = 2
NT = (((1,), (1,)), ((), ()))


def stripes(width):
    step = STRIPE if width % STRIPE == 0 else width
    return [(at, step) for at in range(0, width, step)]


def kernel(n, cores, examples, length, x_hbm, g_hbm, pi_hbm, po_hbm, q_hbm, out_ref,
           x, g, pi, po, q, in_mine, in_peer, outer, share, share_peer, msg, got, entries, wide, part, parts,
           load_sem, in_sem, share_sem, msg_send, msg_recv, part_send, part_recv):
    me = lax.axis_index("dp")
    core = lax.axis_index("tensor")
    rank = pi.shape[0]
    tokens = x.shape[0]
    tile = msg.shape[1]
    pieces = tile // examples
    per_piece = LANES // rank

    loads = []

    def plan(hbm, vmem, row, height, at, size):
        where = (pl.ds(row, height), pl.ds(at, size))
        copy = pltpu.make_async_copy(hbm.at[where], vmem.at[where], load_sem.at[len(loads)])
        loads.append(copy)
        return len(loads) - 1

    in_loads = [(at, size, (plan(pi_hbm, pi, 0, rank, at, size), plan(x_hbm, x, 0, tokens, at, size)))
                for at, size in stripes(x.shape[1])]
    out_loads = [(at, size, (plan(po_hbm, po, 0, rank, at, size), plan(g_hbm, g, 0, tokens, at, size)))
                 for at, size in stripes(g.shape[1])]
    q_load = plan(q_hbm, q, 0, q.shape[0], 0, q.shape[1])

    for copy in loads[:IN_FLIGHT]:
        copy.start()

    def arrive(at):
        loads[at].wait()
        if at + IN_FLIGHT < len(loads):
            loads[at + IN_FLIGHT].start()

    barrier = pltpu.get_barrier_semaphore()
    others = [(k, 0) for k in range(1, n)] + [(0, c) for c in range(1, cores)]

    def device(k, c):
        return {"dp": lax.rem(me + k, n), "tensor": lax.rem(core + c, cores)}

    for k, c in others:
        pl.semaphore_signal(barrier, inc=1, device_id=device(k, c), device_id_type=MESH)

    def by_token(proj, data):
        return lax.dot_general(data, proj, NT, preferred_element_type=jnp.float32)

    def halves(value):
        high = value.astype(jnp.bfloat16)
        return high, (value - high.astype(jnp.float32)).astype(jnp.bfloat16)

    def project(multiply, proj, data, row, height, arrivals):
        total = None
        for at, size, copies in arrivals:
            for copy in copies:
                arrive(copy)
            term = multiply(proj[:, pl.ds(at, size)], data[pl.ds(row, height), pl.ds(at, size)])
            total = term if total is None else total + term
        return total

    mine = project(by_token, pi, x, 0, tokens, in_loads)
    in_mine[...] = jnp.concatenate(
        [mine[e * length:(e + 1) * length] for e in range(examples)], 1)

    before = len(out_loads) // 2
    out_side = project(by_token, po, g, 0, tokens, out_loads[:before]) if before else 0.0
    pl.semaphore_wait(barrier, len(others))

    def swap(source, peers, sems):
        copies = [
            pltpu.make_async_remote_copy(
                src_ref=source, dst_ref=peers.at[c - 1], send_sem=sems.at[0, c - 1],
                recv_sem=sems.at[1, c - 1], device_id=device(0, c), device_id_type=MESH)
            for c in range(1, cores)]
        for copy in copies:
            copy.start()
        return copies

    in_swap = swap(in_mine, in_peer, in_sem)
    out_side = out_side + project(by_token, po, g, 0, tokens, out_loads[before:])
    out_high, out_low = halves(out_side.T)
    in_side = in_mine[...]
    for c, copy in enumerate(in_swap):
        copy.wait()
        in_side = in_side + in_peer[c]
    in_high, in_low = halves(in_side)

    half = rank // per_piece
    for e in range(examples):
        here, there = slice(e * length, (e + 1) * length), slice(e * rank, (e + 1) * rank)
        left_high, left_low = out_high[:, here], out_low[:, here]
        high, low = in_high[:, there], in_low[:, there]
        outer[e] = jnp.dot(jnp.concatenate([left_high, left_high, left_low, left_low], 1),
                           jnp.concatenate([high, low, high, low], 0),
                           preferred_element_type=jnp.float32)
        share[pl.ds(e * half, half), :] = jnp.concatenate(
            [outer[e, pl.ds(i, half, stride=per_piece), :] for i in range(per_piece)], 1)
    share_swap = swap(share, share_peer, share_sem)
    joined = share[...]
    for c, copy in enumerate(share_swap):
        copy.wait()
        joined = joined + share_peer[c]
    joined = joined * (1.0 / length)
    for d in range(n):
        for e in range(examples):
            msg[d, pl.ds(e * pieces, pieces), :] = joined[e * half + d * pieces:e * half + (d + 1) * pieces]
    sends = {}
    for k in sorted(range(1, n), key=lambda k: -min(k, n - k)):
        copy = pltpu.make_async_remote_copy(
            src_ref=msg.at[lax.rem(me + k, n)], dst_ref=got.at[k],
            send_sem=msg_send.at[k], recv_sem=msg_recv.at[k],
            device_id=device(k, 0), device_id_type=MESH)
        copy.start()
        sends[k] = copy
    arrive(q_load)
    entries[pl.ds(0, tile), :] = msg[me]
    for k in range(1, n):
        sends[k].wait_recv()
        entries[pl.ds(k * tile, tile), :] = got[k]
    sketch = jnp.concatenate(
        [jnp.concatenate([entries[pl.ds(e * pieces + j, n, stride=tile), :] for e in range(examples)], 0)
         for j in range(pieces)], 1).astype(jnp.bfloat16)

    chunk = q.shape[0] // QUERY_CHUNKS
    blocks = chunk // LANES
    height = blocks * examples
    final = {}
    for h in range(QUERY_CHUNKS):
        scores = lax.dot_general(sketch, q[pl.ds(h * chunk, chunk), :], NT,
                                 preferred_element_type=jnp.float32)
        for b in range(blocks):
            for e in range(examples):
                wide[h, pl.ds(b * examples + e, n, stride=height), :] = (
                    scores[e * n:(e + 1) * n, b * LANES:(b + 1) * LANES])
        for k in sorted(range(1, n), key=lambda k: -min(k, n - k)):
            part[h, k] = wide[h, pl.ds(k * height, height), :].astype(part.dtype)
            copy = pltpu.make_async_remote_copy(
                src_ref=part.at[h, k], dst_ref=parts.at[h, k],
                send_sem=part_send.at[h, k], recv_sem=part_recv.at[h, k],
                device_id=device(n - k, 0), device_id_type=MESH)
            copy.start()
            final[h, k] = copy
    for h in range(QUERY_CHUNKS):
        total = wide[h, pl.ds(0, height), :]
        for k in range(1, n):
            final[h, k].wait_recv()
            total = total + parts[h, k].astype(jnp.float32)
        out_ref[pl.ds(h * height, height), :] = total
    for copy in list(sends.values()) + list(final.values()):
        copy.wait_send()


def on_device(n, cores, inputs, out_grads, proj_in, proj_out, queries):
    examples, length, d_in = inputs.shape
    d_out = out_grads.shape[2]
    rank = proj_in.shape[1]
    queries_here, entries_here = queries.shape
    tokens = examples * length
    pieces = entries_here // LANES
    out_rows = examples * queries_here // LANES
    blocks = queries_here // QUERY_CHUNKS // LANES
    f32, bf16 = jnp.float32, jnp.bfloat16
    n_loads = 2 * len(stripes(d_in)) + 2 * len(stripes(d_out)) + 1
    dma = pltpu.SemaphoreType.DMA
    flat = pl.pallas_call(
        functools.partial(kernel, n, cores, examples, length),
        out_shape=jax.ShapeDtypeStruct((out_rows, LANES), f32),
        in_specs=[pl.BlockSpec(memory_space=pl.ANY)] * 5,
        out_specs=pl.BlockSpec(memory_space=pltpu.VMEM),
        scratch_shapes=[
            pltpu.VMEM((tokens, d_in), bf16),
            pltpu.VMEM((tokens, d_out), bf16),
            pltpu.VMEM((rank, d_in), bf16),
            pltpu.VMEM((rank, d_out), bf16),
            pltpu.VMEM((queries_here, entries_here), bf16),
            pltpu.VMEM((length, examples * rank), f32),
            pltpu.VMEM((cores - 1, length, examples * rank), f32),
            pltpu.VMEM((examples, rank, rank), f32),
            pltpu.VMEM((examples * pieces * n, LANES), f32),
            pltpu.VMEM((cores - 1, examples * pieces * n, LANES), f32),
            pltpu.VMEM((n, examples * pieces, LANES), f32),
            pltpu.VMEM((n, examples * pieces, LANES), f32),
            pltpu.VMEM((n * examples * pieces, LANES), f32),
            pltpu.VMEM((QUERY_CHUNKS, n * examples * blocks, LANES), f32),
            pltpu.VMEM((QUERY_CHUNKS, n, examples * blocks, LANES), bf16),
            pltpu.VMEM((QUERY_CHUNKS, n, examples * blocks, LANES), bf16),
            dma((n_loads,)),
            dma((2, cores - 1)),
            dma((2, cores - 1)),
            dma((n,)),
            dma((n,)),
            dma((QUERY_CHUNKS, n)),
            dma((QUERY_CHUNKS, n)),
        ],
        compiler_params=pltpu.CompilerParams(
            collective_id=0, has_side_effects=True, vmem_limit_bytes=60 * 2**20),
    )(inputs.reshape(tokens, d_in), out_grads.reshape(tokens, d_out), proj_in.T, proj_out.T, queries)
    return flat.reshape(queries_here // LANES, examples, LANES).transpose(1, 0, 2).reshape(
        examples, queries_here)


def solution(mesh):
    return jax.shard_map(
        functools.partial(on_device, mesh.shape["dp"], mesh.shape["tensor"]),
        mesh=mesh,
        in_specs=(
            P(("groups", "dp"), None, "tensor"),
            P(("groups", "dp"), None, "tensor"),
            P("tensor", None),
            P("tensor", None),
            P("tensor", "dp"),
        ),
        out_specs=P(("groups", "dp"), "tensor"),
        check_vma=False,
    )
```

```python
import functools

import jax
import jax.numpy as jnp
from jax import lax
from jax.experimental import pallas as pl
from jax.experimental.pallas import tpu as pltpu
from jax.sharding import PartitionSpec as P

MESH = pl.DeviceIdType.MESH
LANES = 128
STRIPE = 2048
IN_FLIGHT = 100
QUERY_CHUNKS = 2
NT = (((1,), (1,)), ((), ()))


def stripes(width):
    step = STRIPE if width % STRIPE == 0 else width
    return [(at, step) for at in range(0, width, step)]


def kernel(n, cores, examples, length, x_hbm, g_hbm, pi_hbm, po_hbm, q_hbm, out_ref,
           x, g, pi, po, q, in_mine, in_peer, outer, share, share_peer, msg, got, entries, wide, part, parts,
           load_sem, in_sem, share_sem, msg_send, msg_recv, part_send, part_recv):
    me = lax.axis_index("dp")
    core = lax.axis_index("tensor")
    rank = pi.shape[0]
    tokens = x.shape[0]
    tile = msg.shape[1]
    pieces = tile // examples
    per_piece = LANES // rank

    loads = []

    def plan(hbm, vmem, row, height, at, size):
        where = (pl.ds(row, height), pl.ds(at, size))
        copy = pltpu.make_async_copy(hbm.at[where], vmem.at[where], load_sem.at[len(loads)])
        loads.append(copy)
        return len(loads) - 1

    in_loads = [(at, size, (plan(pi_hbm, pi, 0, rank, at, size), plan(x_hbm, x, 0, tokens, at, size)))
                for at, size in stripes(x.shape[1])]
    out_loads = [(at, size, (plan(po_hbm, po, 0, rank, at, size), plan(g_hbm, g, 0, tokens, at, size)))
                 for at, size in stripes(g.shape[1])]
    q_load = plan(q_hbm, q, 0, q.shape[0], 0, q.shape[1])

    for copy in loads[:IN_FLIGHT]:
        copy.start()

    def arrive(at):
        loads[at].wait()
        if at + IN_FLIGHT < len(loads):
            loads[at + IN_FLIGHT].start()

    barrier = pltpu.get_barrier_semaphore()
    others = [(k, 0) for k in range(1, n)] + [(0, c) for c in range(1, cores)]

    def device(k, c):
        return {"dp": lax.rem(me + k, n), "tensor": lax.rem(core + c, cores)}

    for k, c in others:
        pl.semaphore_signal(barrier, inc=1, device_id=device(k, c), device_id_type=MESH)

    def by_token(proj, data):
        return lax.dot_general(data, proj, NT, preferred_element_type=jnp.float32)

    def halves(value):
        high = value.astype(jnp.bfloat16)
        return high, (value - high.astype(jnp.float32)).astype(jnp.bfloat16)

    def project(multiply, proj, data, row, height, arrivals):
        total = None
        for at, size, copies in arrivals:
            for copy in copies:
                arrive(copy)
            term = multiply(proj[:, pl.ds(at, size)], data[pl.ds(row, height), pl.ds(at, size)])
            total = term if total is None else total + term
        return total

    mine = project(by_token, pi, x, 0, tokens, in_loads)
    in_mine[...] = jnp.concatenate(
        [mine[e * length:(e + 1) * length] for e in range(examples)], 1)

    before = max(len(out_loads) - 2, 0)
    out_side = project(by_token, po, g, 0, tokens, out_loads[:before]) if before else 0.0
    pl.semaphore_wait(barrier, len(others))

    def swap(source, peers, sems):
        copies = [
            pltpu.make_async_remote_copy(
                src_ref=source, dst_ref=peers.at[c - 1], send_sem=sems.at[0, c - 1],
                recv_sem=sems.at[1, c - 1], device_id=device(0, c), device_id_type=MESH)
            for c in range(1, cores)]
        for copy in copies:
            copy.start()
        return copies

    in_swap = swap(in_mine, in_peer, in_sem)
    out_side = out_side + project(by_token, po, g, 0, tokens, out_loads[before:])
    out_high, out_low = halves(out_side.T)
    in_side = in_mine[...]
    for c, copy in enumerate(in_swap):
        copy.wait()
        in_side = in_side + in_peer[c]
    in_high, in_low = halves(in_side)

    half = rank // per_piece
    for e in range(examples):
        here, there = slice(e * length, (e + 1) * length), slice(e * rank, (e + 1) * rank)
        left_high, left_low = out_high[:, here], out_low[:, here]
        high, low = in_high[:, there], in_low[:, there]
        outer[e] = jnp.dot(jnp.concatenate([left_high, left_high, left_low, left_low], 1),
                           jnp.concatenate([high, low, high, low], 0),
                           preferred_element_type=jnp.float32)
        share[pl.ds(e * half, half), :] = jnp.concatenate(
            [outer[e, pl.ds(i, half, stride=per_piece), :] for i in range(per_piece)], 1)
    share_swap = swap(share, share_peer, share_sem)
    joined = share[...]
    for c, copy in enumerate(share_swap):
        copy.wait()
        joined = joined + share_peer[c]
    joined = joined * (1.0 / length)
    for d in range(n):
        for e in range(examples):
            msg[d, pl.ds(e * pieces, pieces), :] = joined[e * half + d * pieces:e * half + (d + 1) * pieces]
    sends = {}
    for k in sorted(range(1, n), key=lambda k: -min(k, n - k)):
        copy = pltpu.make_async_remote_copy(
            src_ref=msg.at[lax.rem(me + k, n)], dst_ref=got.at[k],
            send_sem=msg_send.at[k], recv_sem=msg_recv.at[k],
            device_id=device(k, 0), device_id_type=MESH)
        copy.start()
        sends[k] = copy
    arrive(q_load)
    entries[pl.ds(0, tile), :] = msg[me]
    for k in range(1, n):
        sends[k].wait_recv()
        entries[pl.ds(k * tile, tile), :] = got[k]
    sketch = jnp.concatenate(
        [jnp.concatenate([entries[pl.ds(e * pieces + j, n, stride=tile), :] for e in range(examples)], 0)
         for j in range(pieces)], 1).astype(jnp.bfloat16)

    chunk = q.shape[0] // QUERY_CHUNKS
    blocks = chunk // LANES
    height = blocks * examples
    final = {}
    for h in range(QUERY_CHUNKS):
        scores = lax.dot_general(sketch, q[pl.ds(h * chunk, chunk), :], NT,
                                 preferred_element_type=jnp.float32)
        for b in range(blocks):
            for e in range(examples):
                wide[h, pl.ds(b * examples + e, n, stride=height), :] = (
                    scores[e * n:(e + 1) * n, b * LANES:(b + 1) * LANES])
        for k in sorted(range(1, n), key=lambda k: -min(k, n - k)):
            part[h, k] = wide[h, pl.ds(k * height, height), :].astype(part.dtype)
            copy = pltpu.make_async_remote_copy(
                src_ref=part.at[h, k], dst_ref=parts.at[h, k],
                send_sem=part_send.at[h, k], recv_sem=part_recv.at[h, k],
                device_id=device(n - k, 0), device_id_type=MESH)
            copy.start()
            final[h, k] = copy
    for h in range(QUERY_CHUNKS):
        total = wide[h, pl.ds(0, height), :]
        for k in range(1, n):
            final[h, k].wait_recv()
            total = total + parts[h, k].astype(jnp.float32)
        out_ref[pl.ds(h * height, height), :] = total
    for copy in list(sends.values()) + list(final.values()):
        copy.wait_send()


def on_device(n, cores, inputs, out_grads, proj_in, proj_out, queries):
    examples, length, d_in = inputs.shape
    d_out = out_grads.shape[2]
    rank = proj_in.shape[1]
    queries_here, entries_here = queries.shape
    tokens = examples * length
    pieces = entries_here // LANES
    out_rows = examples * queries_here // LANES
    blocks = queries_here // QUERY_CHUNKS // LANES
    f32, bf16 = jnp.float32, jnp.bfloat16
    n_loads = 2 * len(stripes(d_in)) + 2 * len(stripes(d_out)) + 1
    dma = pltpu.SemaphoreType.DMA
    flat = pl.pallas_call(
        functools.partial(kernel, n, cores, examples, length),
        out_shape=jax.ShapeDtypeStruct((out_rows, LANES), f32),
        in_specs=[pl.BlockSpec(memory_space=pl.ANY)] * 5,
        out_specs=pl.BlockSpec(memory_space=pltpu.VMEM),
        scratch_shapes=[
            pltpu.VMEM((tokens, d_in), bf16),
            pltpu.VMEM((tokens, d_out), bf16),
            pltpu.VMEM((rank, d_in), bf16),
            pltpu.VMEM((rank, d_out), bf16),
            pltpu.VMEM((queries_here, entries_here), bf16),
            pltpu.VMEM((length, examples * rank), f32),
            pltpu.VMEM((cores - 1, length, examples * rank), f32),
            pltpu.VMEM((examples, rank, rank), f32),
            pltpu.VMEM((examples * pieces * n, LANES), f32),
            pltpu.VMEM((cores - 1, examples * pieces * n, LANES), f32),
            pltpu.VMEM((n, examples * pieces, LANES), f32),
            pltpu.VMEM((n, examples * pieces, LANES), f32),
            pltpu.VMEM((n * examples * pieces, LANES), f32),
            pltpu.VMEM((QUERY_CHUNKS, n * examples * blocks, LANES), f32),
            pltpu.VMEM((QUERY_CHUNKS, n, examples * blocks, LANES), bf16),
            pltpu.VMEM((QUERY_CHUNKS, n, examples * blocks, LANES), bf16),
            dma((n_loads,)),
            dma((2, cores - 1)),
            dma((2, cores - 1)),
            dma((n,)),
            dma((n,)),
            dma((QUERY_CHUNKS, n)),
            dma((QUERY_CHUNKS, n)),
        ],
        compiler_params=pltpu.CompilerParams(
            collective_id=0, has_side_effects=True, vmem_limit_bytes=60 * 2**20),
    )(inputs.reshape(tokens, d_in), out_grads.reshape(tokens, d_out), proj_in.T, proj_out.T, queries)
    return flat.reshape(queries_here // LANES, examples, LANES).transpose(1, 0, 2).reshape(
        examples, queries_here)


def solution(mesh):
    return jax.shard_map(
        functools.partial(on_device, mesh.shape["dp"], mesh.shape["tensor"]),
        mesh=mesh,
        in_specs=(
            P(("groups", "dp"), None, "tensor"),
            P(("groups", "dp"), None, "tensor"),
            P("tensor", None),
            P("tensor", None),
            P("tensor", "dp"),
        ),
        out_specs=P(("groups", "dp"), "tensor"),
        check_vma=False,
    )
```
